1024 devices in a mesh: row: 128 (over z_lo, y, core), rep: 8 (over z_hi, x).
Axes of the slice: x: 4, y: 8, z: 16 (z_hi: 2, z_lo: 8; z = z_hi * 8 + z_lo), core: 2. Of those that a mesh axis runs over, the one named last changes fastest.
Arguments:
- features: bfloat16 [262144, 128], P('row'), may hold values from -6 to 6
- weight: bfloat16 [128, 256], replicated, may hold values from -0.5 to 0.5
- section_source: int32 [16], P('rep'), may hold values from 0 to 127, as said below
- tile_columns: int32 [16, 2048, 3], P('rep', 'row'), may hold values from 0 to 15, as said below
- tile_counts: int32 [16, 2048], P('rep', 'row'), may hold values from 1 to 3
- tile_values: bfloat16 [16, 2048, 3, 128, 128], P('rep', 'row'), may hold values from 0.001876831 to 0.037353516
- cotangent: bfloat16 [262144, 256], P('row'), may hold values from -0.01171875 to 0.01171875
Outputs:
- activations: bfloat16 [262144, 256], P(('row', 'rep'))
- weight_grad: float32 [128, 256], replicated
The draws below stay inside these ranges and needn't reach their ends.
Inputs may be any that keep to these rules, and one draw needn't show every extreme that they name: `section_source`: the 16 entries are distinct row groups. `tile_columns`: within one section and node block, the 3 slots name distinct blocks; slots from tile_counts on are ignored.
All inputs are finite; a program needn't handle non-finite values.
Results may differ from the reference program's by a relative error of at most 0.0053.
Values may be sent and summed in bfloat16 or wider, within the bound.
A program may use at most 32 MiB of HBM per device.

```python
import math
import jax
import jax.numpy as jnp
from jax import lax

FEAT_IN = 128
HIDDEN_SIZE = 256
TILE = 128
GROUP_BLOCKS = 16
MAX_TILES = 3
SECTIONS = 16
NBLOCKS = 2048
NODES = 262144
N_ROW = 128


def draw_section_source(key, part):
    key = jax.random.fold_in(key, 11)
    first_key, second_key = jax.random.split(key)
    middle = jax.random.permutation(first_key, N_ROW - 2).astype(jnp.int32) + 1
    chosen = jnp.concatenate([jnp.array([N_ROW - 1, 0], jnp.int32), middle[:SECTIONS - 2]])
    return jax.random.permutation(second_key, chosen).astype(jnp.int32)


def draw_tile_columns(key, part):
    key = jax.random.fold_in(key, 13)
    keys = jax.random.split(key, 4)
    offset = jax.random.randint(keys[0], (SECTIONS, NBLOCKS, 1), 0, GROUP_BLOCKS)
    stride = 2 * jax.random.randint(keys[1], (SECTIONS, NBLOCKS, 1), 0, GROUP_BLOCKS // 2) + 1
    section_pick = jax.random.randint(keys[2], (), 0, SECTIONS)
    block_pick = jax.random.randint(keys[3], (), 0, NBLOCKS)
    offset = offset.at[section_pick, block_pick, 0].set(GROUP_BLOCKS - 1)
    offset = offset.at[(section_pick + 1) % SECTIONS, block_pick, 0].set(0)
    slot_index = jnp.arange(MAX_TILES, dtype=jnp.int32)[None, None, :]
    return ((offset + stride * slot_index) % GROUP_BLOCKS).astype(jnp.int32)


def draw_tile_counts(key, part):
    key = jax.random.fold_in(key, 17)
    keys = jax.random.split(key, 3)
    counts = jax.random.randint(keys[0], (SECTIONS, NBLOCKS), 1, MAX_TILES + 1)
    section_pick = jax.random.randint(keys[1], (), 0, SECTIONS)
    block_pick = jax.random.randint(keys[2], (), 0, NBLOCKS)
    counts = counts.at[section_pick, block_pick].set(MAX_TILES)
    counts = counts.at[(section_pick + 1) % SECTIONS, block_pick].set(1)
    return counts.astype(jnp.int32)


def levels(rng, extent, cuts, smallest, top_value):
    def one(position, parts):
        heights = jax.random.uniform(jax.random.fold_in(jax.random.fold_in(rng, 6), position), (parts,), jnp.float32, smallest / len(cuts), top_value / len(cuts))
        return jnp.repeat(jnp.exp(heights), extent[position] // parts).reshape((-1,) + (1,) * (len(extent) - position - 1))

    factor_of = one(*cuts[0])
    for cut in cuts[1:]:
        factor_of = factor_of * one(*cut)
    return factor_of


def gaussian(key, shape, deviation, reach, cuts=(), kind=jnp.bfloat16):
    loudness = levels(key, shape, cuts, -0.22, 0.18) if cuts else 1.0
    values = jax.random.normal(key, shape, jnp.float32) * deviation * loudness
    return jnp.minimum(jnp.maximum(values, -reach), reach).astype(kind)


def setup_inputs(seed: int = 0) -> dict:
    key_of = jax.random.split(jax.random.key(seed), 8)
    return {
        "features": gaussian(key_of[0], (NODES, FEAT_IN), 1.0, 6.0, ((0, 128),)),
        "weight": gaussian(key_of[1], (FEAT_IN, HIDDEN_SIZE), FEAT_IN ** -0.5, 0.5),
        "section_source": draw_section_source(jax.random.fold_in(key_of[7], 71), 0),
        "tile_columns": draw_tile_columns(jax.random.fold_in(key_of[7], 71), 0),
        "tile_counts": draw_tile_counts(jax.random.fold_in(key_of[7], 71), 0),
        "tile_values": jnp.clip(jnp.exp(math.log(0.037353516) - 2.9908423 * jax.random.uniform(key_of[5], (SECTIONS, NBLOCKS, MAX_TILES, TILE, TILE), jnp.float32) ** levels(key_of[5], (SECTIONS, NBLOCKS, MAX_TILES, TILE, TILE), ((0, 8), (1, 128)), -0.2, 0.2)), 0.001876831, 0.037353516).astype(jnp.bfloat16),
        "cotangent": gaussian(key_of[6], (NODES, HIDDEN_SIZE), (NODES ** -0.5), 0.01171875, ((0, 128),)),
    }


def reference(features, weight, section_source, tile_columns, tile_counts, tile_values, cotangent):
    blocks_all = features.reshape(NBLOCKS, TILE, FEAT_IN)
    slot_index = jnp.arange(MAX_TILES, dtype=jnp.int32)

    def one_section(carry, inputs):
        source_group, columns, counts, values = inputs
        source_ids = (source_group * GROUP_BLOCKS + columns).astype(jnp.int32)
        picked = jnp.take(blocks_all, source_ids, axis=0).astype(jnp.float32)
        live_slot = slot_index[None, :] < counts[:, None]
        tile_data = jnp.where(live_slot[:, :, None, None], values.astype(jnp.float32), 0.0)
        term = jnp.einsum("bmij,bmjf->bif", tile_data, picked)
        return carry + term, None

    start = jnp.zeros((NBLOCKS, TILE, FEAT_IN), jnp.float32)
    summed, _ = lax.scan(one_section, start, (section_source, tile_columns, tile_counts, tile_values))
    aggregate = summed.reshape(NODES, FEAT_IN).astype(jnp.bfloat16)
    preact = jnp.dot(aggregate, weight, preferred_element_type=jnp.float32)
    sigmoid_v = jax.nn.sigmoid(preact)
    activations = (preact * sigmoid_v).astype(jnp.bfloat16)
    slope_v = sigmoid_v * (1.0 + preact * (1.0 - sigmoid_v))
    pre_grad = (cotangent.astype(jnp.float32) * slope_v).astype(jnp.bfloat16)
    weight_grad = lax.dot_general(aggregate, pre_grad, (((0,), (0,)), ((), ())), preferred_element_type=jnp.float32)
    return activations, weight_grad
```

```python
import functools

import jax
import jax.numpy as jnp
from jax import lax
from jax.experimental import pallas as pl
from jax.experimental.pallas import tpu as pltpu
from jax.sharding import PartitionSpec as P

MESH = pl.DeviceIdType.MESH
BF16, F32 = jnp.bfloat16, jnp.float32

NZ, NY, NC, NH, NX = 8, 8, 2, 2, 4
ROW_SUM = F32
HALF_SUM = F32
GRAD_A = BF16
GRAD_B = F32


def remote(src, dst, sems, slot, row, rep):
    send, recv = sems
    return pltpu.make_async_remote_copy(
        src_ref=src,
        dst_ref=dst,
        send_sem=send.at[slot],
        recv_sem=recv.at[slot],
        device_id={"row": row, "rep": rep},
        device_id_type=MESH,
    )


def kernel(
    source_ref,
    column_ref,
    count_ref,
    weight_ref,
    features_ref,
    tiles_ref,
    cotangent_ref,
    act_ref,
    grad_ref,
    tiles,
    cot,
    ids,
    cand,
    pick,
    pieces,
    zcand,
    gathered,
    agg,
    xsum,
    own,
    zsum,
    zsend,
    wsend,
    wrecv,
    xgrad,
    zgrad,
    wfull,
    local_sem,
    *sems,
):
    nq = NY * NC
    section_count, block_count, slot_count = tiles.shape[:3]
    sa, si, sx, sr, sg, sy, sc, sp, sh, sw, sv, su, so = [
        (sems[2 * i], sems[2 * i + 1]) for i in range(13)
    ]
    row, rep = lax.axis_index("row"), lax.axis_index("rep")
    zl, q = row // nq, row % nq
    y, c = q // NC, q % NC
    zh, x = rep // NX, rep % NX
    z = zh * NZ + zl

    def q_at(d):
        dy, dc = d // NC, d % NC
        return ((y + dy) % NY) * NC + (c + dc) % NC

    def row_q(d):
        return zl * nq + q_at(d)

    def rep_x(d):
        return zh * NX + (x + d) % NX

    def zlo_at(d):
        return (zl + d) % NZ

    def z_pos(d):
        return (z + d) % (NZ * NH)

    def z_dev(d):
        zz = z_pos(d)
        return (zz % NZ) * nq + q, (zz // NZ) * NX + x

    tile_copy = pltpu.make_async_copy(tiles_ref, tiles, local_sem.at[0])
    tile_copy.start()
    own_rows = cot.shape[0]
    cot_copy = pltpu.make_async_copy(
        cotangent_ref.at[pl.ds(pl.multiple_of(rep * own_rows, own_rows), own_rows)],
        cot,
        local_sem.at[1],
    )
    cot_copy.start()

    barrier = pltpu.get_barrier_semaphore()
    peers = [(row_q(d), rep) for d in range(1, nq)]
    peers += [(row, rep_x(d)) for d in range(1, NX)]
    peers += [z_dev(d) for d in range(1, NZ * NH)]
    for r, p in peers:
        pl.semaphore_signal(
            barrier, inc=1, device_id={"row": r, "rep": p}, device_id_type=MESH
        )

    for k in range(section_count):
        ids[x, k] = jnp.full(ids.shape[2:], (source_ref[k] % nq).astype(F32)).astype(BF16)
    gathered[:, block_count] = jnp.zeros(
        (section_count,) + gathered.shape[2:], BF16
    )

    pl.semaphore_wait(barrier, len(peers))

    pending = []

    per_x = NZ // NX

    def rows_for(dq):
        return features_ref.at[pl.ds(dq * NZ + x * per_x, per_x)]

    id_copies = []
    for d in range(1, NX):
        copy = remote(ids.at[x], ids.at[x], si, d, row, rep_x(d))
        copy.start()
        id_copies.append(copy)
    a_copies = []
    for d in range(1, nq):
        copy = remote(rows_for(q_at(d)), cand.at[q], sa, d, row_q(d), rep)
        copy.start()
        a_copies.append(copy)
    own_copy = pltpu.make_async_copy(rows_for(q), cand.at[q], local_sem.at[2])
    own_copy.start()
    own_copy.wait()
    for copy in id_copies + a_copies:
        copy.wait_recv()
    pending += id_copies + a_copies

    x_copies = []
    for d in list(range(1, NX)) + [0]:
        tx = (x + d) % NX
        for k in range(section_count):
            want = ids[tx, k][None]
            chosen = cand[0]
            for s in range(1, nq):
                chosen = jnp.where(want == jnp.asarray(s, BF16), cand[s], chosen)
            if d == 0:
                pieces[k, pl.ds(x * per_x, per_x)] = chosen
            else:
                pick[d, k] = chosen
        if d != 0:
            copy = remote(
                pick.at[d], pieces.at[:, pl.ds(x * per_x, per_x)], sx, d, row, rep_x(d)
            )
            copy.start()
            x_copies.append(copy)
    for copy in x_copies:
        copy.wait_recv()
    pending += x_copies

    r_copies = []
    for d in range(1, NZ):
        t = zlo_at(d)
        copy = remote(pieces.at[:, t], zcand.at[zl], sr, d, t * nq + q, rep)
        copy.start()
        r_copies.append(copy)
    zcand[zl] = pieces[:, zl]
    for copy in r_copies:
        copy.wait_recv()
    pending += r_copies
    for k in range(section_count):
        gathered[k, q, zl] = zcand[source_ref[k] // nq, k]

    g_copies = []
    for d in range(1, NZ):
        t = zlo_at(d)
        mine = gathered.at[:, q, zl]
        copy = remote(mine, mine, sg, d, t * nq + q, rep)
        copy.start()
        g_copies.append(copy)
    for copy in g_copies:
        copy.wait_recv()
    pending += g_copies

    block = gathered.at[:, q]
    sib_row = row_q(1) if NC == 2 else row
    y_copies = []
    for dy in range(1, NY):
        copy = remote(block, block, sy, dy, row_q(dy * NC), rep)
        copy.start()
        y_copies.append(copy)
    c_copies = []
    for dy in range(NY):
        if dy > 0:
            y_copies[dy - 1].wait_recv()
        got = gathered.at[:, q_at(((NY - dy) % NY) * NC)]
        copy = remote(got, got, sc, dy, sib_row, rep)
        copy.start()
        c_copies.append(copy)
    for copy in c_copies:
        copy.wait_recv()
    pending += y_copies + c_copies

    tile_copy.wait()
    per_owner = block_count // (NH * NX)
    edge = agg.shape[-1]

    def product(b):
        left, right = [], []
        for k in range(section_count):
            for m in range(slot_count):
                live = m < count_ref[k, b]
                col = jnp.where(live, column_ref[k, b, m], block_count)
                left.append(tiles[k, b, m])
                right.append(gathered[k, col].reshape(edge, edge))
        return jnp.dot(
            jnp.concatenate(left, axis=1),
            jnp.concatenate(right, axis=0),
            preferred_element_type=F32,
        )

    p_copies = []
    for d in list(range(1, NX)) + [0]:
        tx = (x + d) % NX
        for h in range(NH):
            def one(j, _, tx=tx, h=h):
                value = product((h * NX + tx) * per_owner + j)
                if d == 0:
                    own[h, j] = value
                else:
                    agg[d, h, j] = value.astype(ROW_SUM)
                return _

            lax.fori_loop(0, per_owner, one, 0)
        if d != 0:
            copy = remote(agg.at[d], xsum.at[d], sp, d, row, rep_x(d))
            copy.start()
            p_copies.append(copy)
    for copy in p_copies:
        copy.wait_recv()
    pending += p_copies

    def total(h):
        out = own[h]
        for d in range(1, NX):
            out = out + xsum[d, h].astype(F32)
        return out

    if NH == 2:
        zsend[...] = total(1 - zh).astype(HALF_SUM)
        partner = z_dev(NZ)
        h_copy = remote(zsend, zsum, sh, 0, partner[0], partner[1])
        h_copy.start()
        kept = total(zh)
        h_copy.wait_recv()
        pending.append(h_copy)
        summed = kept + zsum[...].astype(F32)
    else:
        summed = total(0)
    aggregate = summed.reshape(own_rows, edge).astype(BF16)

    preact = jnp.dot(aggregate, weight_ref[...], preferred_element_type=F32)
    sigmoid = jax.nn.sigmoid(preact)
    act_ref[...] = (preact * sigmoid).astype(BF16)
    slope = sigmoid * (1.0 + preact * (1.0 - sigmoid))
    cot_copy.wait()
    pre_grad = (cot[...].astype(F32) * slope).astype(BF16)
    part = lax.dot_general(
        aggregate, pre_grad, (((0,), (0,)), ((), ())), preferred_element_type=F32
    )
    tall, wide = wsend.shape[1:]
    across = part.shape[1] // wide
    for t in range(nq):
        top, left = (t // across) * tall, (t % across) * wide
        wsend[t] = part[top : top + tall, left : left + wide].astype(GRAD_A)

    w_copies = []
    for d in range(1, nq):
        copy = remote(wsend.at[q_at(d)], wrecv.at[q], sw, d, row_q(d), rep)
        copy.start()
        w_copies.append(copy)
    wrecv[q] = wsend[q]
    for copy in w_copies:
        copy.wait_recv()
    pending += w_copies
    xgrad[x] = functools.reduce(
        lambda a, b: a + b, [wrecv[t].astype(F32) for t in range(nq)]
    ).astype(GRAD_B)
    v_copies = []
    for d in range(1, NX):
        copy = remote(xgrad.at[x], xgrad.at[x], sv, d, row, rep_x(d))
        copy.start()
        v_copies.append(copy)
    for copy in v_copies:
        copy.wait_recv()
    pending += v_copies
    zgrad[z] = functools.reduce(
        lambda a, b: a + b, [xgrad[t].astype(F32) for t in range(NX)]
    ).astype(GRAD_B)
    u_copies = []
    for d in range(1, NZ * NH):
        r, p = z_dev(d)
        copy = remote(zgrad.at[z], zgrad.at[z], su, d, r, p)
        copy.start()
        u_copies.append(copy)
    for copy in u_copies:
        copy.wait_recv()
    pending += u_copies
    wfull[q] = functools.reduce(
        lambda a, b: a + b, [zgrad[t].astype(F32) for t in range(NZ * NH)]
    ).astype(GRAD_B)
    o_copies = []
    for d in range(1, nq):
        copy = remote(wfull.at[q], wfull.at[q], so, d, row_q(d), rep)
        copy.start()
        o_copies.append(copy)
    for copy in o_copies:
        copy.wait_recv()
    pending += o_copies
    for t in range(nq):
        top, left = (t // across) * tall, (t % across) * wide
        grad_ref[top : top + tall, left : left + wide] = wfull[t].astype(F32)

    for copy in pending:
        copy.wait_send()


def body(features, weight, section_source, tile_columns, tile_counts, tile_values, cotangent):
    rows, width = features.shape
    sections, blocks, slots, edge, _ = tile_values.shape
    hidden = weight.shape[1]
    nq = NY * NC
    piece = edge // NZ
    own_rows = rows // (NH * NX)
    per_owner = blocks // (NH * NX)
    per_x = NZ // NX
    tall = width * (hidden // edge) // nq
    dma = pltpu.SemaphoreType.DMA
    counts = [nq, NX, NX, NZ, NZ, NY, NY, NX, 1, nq, NX, NZ * NH, nq]
    smem = pl.BlockSpec(memory_space=pltpu.SMEM)
    vmem = pl.BlockSpec(memory_space=pltpu.VMEM)
    hbm = pl.BlockSpec(memory_space=pltpu.HBM)
    return pl.pallas_call(
        kernel,
        out_shape=(
            jax.ShapeDtypeStruct((own_rows, hidden), BF16),
            jax.ShapeDtypeStruct((width, hidden), F32),
        ),
        in_specs=[smem, smem, smem, vmem, hbm, hbm, hbm],
        out_specs=(vmem, vmem),
        scratch_shapes=[
            pltpu.VMEM(tile_values.shape, BF16),
            pltpu.VMEM((own_rows, hidden), BF16),
            pltpu.VMEM((NX, sections, piece, width), BF16),
            pltpu.VMEM((nq, per_x, piece, width), BF16),
            pltpu.VMEM((NX, sections, per_x, piece, width), BF16),
            pltpu.VMEM((sections, NZ, piece, width), BF16),
            pltpu.VMEM((NZ, sections, piece, width), BF16),
            pltpu.VMEM((sections, blocks + 1, NZ, piece, width), BF16),
            pltpu.VMEM((NX, NH, per_owner, edge, width), ROW_SUM),
            pltpu.VMEM((NX, NH, per_owner, edge, width), ROW_SUM),
            pltpu.VMEM((NH, per_owner, edge, width), F32),
            pltpu.VMEM((per_owner, edge, width), HALF_SUM),
            pltpu.VMEM((per_owner, edge, width), HALF_SUM),
            pltpu.VMEM((nq, tall, edge), GRAD_A),
            pltpu.VMEM((nq, tall, edge), GRAD_A),
            pltpu.VMEM((NX, tall, edge), GRAD_B),
            pltpu.VMEM((NZ * NH, tall, edge), GRAD_B),
            pltpu.VMEM((nq, tall, edge), GRAD_B),
            dma((3,)),
        ]
        + [dma((n,)) for n in counts for _ in range(2)],
        compiler_params=pltpu.CompilerParams(
            collective_id=0, has_side_effects=True, vmem_limit_bytes=48 * 1024 * 1024
        ),
        cost_estimate=pl.CostEstimate(
            flops=2 * sections * blocks * slots * edge * edge * width,
            bytes_accessed=tile_values.size * 2,
            transcendentals=own_rows * hidden,
        ),
    )(
        section_source,
        tile_columns,
        tile_counts,
        weight,
        features.reshape(rows // piece, piece, width),
        tile_values,
        cotangent,
    )


def solution(mesh):
    in_specs = (
        P("row", None),
        P(),
        P("rep"),
        P("rep", "row", None),
        P("rep", "row"),
        P("rep", "row", None, None, None),
        P("row", None),
    )
    out_specs = (P(("row", "rep"), None), P())
    return jax.shard_map(body, mesh=mesh, in_specs=in_specs, out_specs=out_specs, check_vma=False)
```

```python
import functools

import jax
import jax.numpy as jnp
from jax import lax
from jax.experimental import pallas as pl
from jax.experimental.pallas import tpu as pltpu
from jax.sharding import PartitionSpec as P

MESH = pl.DeviceIdType.MESH
BF16, F32 = jnp.bfloat16, jnp.float32

NZ, NY, NC, NH, NX = 8, 8, 2, 2, 4
ROW_SUM = BF16
HALF_SUM = BF16
GRAD_A = BF16
GRAD_B = F32


def remote(src, dst, sems, slot, row, rep):
    send, recv = sems
    return pltpu.make_async_remote_copy(
        src_ref=src,
        dst_ref=dst,
        send_sem=send.at[slot],
        recv_sem=recv.at[slot],
        device_id={"row": row, "rep": rep},
        device_id_type=MESH,
    )


def kernel(
    source_ref,
    column_ref,
    count_ref,
    weight_hbm,
    features_ref,
    tiles_ref,
    cotangent_ref,
    act_ref,
    grad_ref,
    tiles,
    cot,
    weight_ref,
    ids,
    cand,
    pick,
    pieces,
    zcand,
    held,
    gathered,
    agg,
    xsum,
    own,
    zsum,
    zsend,
    wsend,
    wrecv,
    xgrad,
    zgrad,
    wfull,
    local_sem,
    far_sem,
    *sems,
):
    nq = NY * NC
    section_count, block_count, slot_count = tiles.shape[:3]
    sa, si, sx, sr, sg, sy, sc, sp, sh, sw, sv, su, so = [
        (sems[2 * i], sems[2 * i + 1]) for i in range(13)
    ]
    row, rep = lax.axis_index("row"), lax.axis_index("rep")
    zl, q = row // nq, row % nq
    y, c = q // NC, q % NC
    zh, x = rep // NX, rep % NX
    z = zh * NZ + zl

    def q_at(d):
        dy, dc = d // NC, d % NC
        return ((y + dy) % NY) * NC + (c + dc) % NC

    def row_q(d):
        return zl * nq + q_at(d)

    def rep_x(d):
        return zh * NX + (x + d) % NX

    def z_pos(d):
        return (z + d + NZ * NH) % (NZ * NH)

    def z_dev(d):
        zz = z_pos(d)
        return (zz % NZ) * nq + q, (zz // NZ) * NX + x

    barrier = pltpu.get_barrier_semaphore()
    peers = [(row_q(d), rep) for d in range(1, nq)]
    peers += [(row, rep_x(d)) for d in range(1, NX)]
    half = NZ // 2
    close = [d for n in range(1, half + 1) for d in (-n, n)]
    peers += [z_dev(d) for d in close]
    over = (zl // half) * NZ - half
    over_row, over_rep = z_dev(over)
    over_h = over_rep // NX
    peers += [(over_row, over_h * NX + (x + d) % NX) for d in range(1, NX)]
    for r, p in peers:
        pl.semaphore_signal(
            barrier, inc=1, device_id={"row": r, "rep": p}, device_id_type=MESH
        )

    tile_copy = pltpu.make_async_copy(tiles_ref, tiles, local_sem.at[0])
    tile_copy.start()
    own_rows = cot.shape[0]
    cot_copy = pltpu.make_async_copy(
        cotangent_ref.at[pl.ds(pl.multiple_of(rep * own_rows, own_rows), own_rows)],
        cot,
        local_sem.at[1],
    )
    cot_copy.start()
    weight_copy = pltpu.make_async_copy(weight_hbm, weight_ref, local_sem.at[3])
    weight_copy.start()

    piece = ids.shape[2]
    share_rows = piece // section_count
    which = lax.broadcasted_iota(jnp.int32, ids.shape[2:], 0) // share_rows
    mixed = jnp.zeros(ids.shape[2:], jnp.int32)
    for k in range(section_count):
        mixed = jnp.where(which == k, source_ref[k], mixed)
    ids[zh, x] = mixed.astype(F32).astype(BF16)
    gathered[:, block_count] = jnp.zeros(
        (section_count,) + gathered.shape[2:], BF16
    )

    pl.semaphore_wait(barrier, len(peers))

    pending = []

    per_x = NZ // NX

    def rows_for(dq):
        return features_ref.at[pl.ds(dq * NZ + x * per_x, per_x)]

    own_ids = ids.at[zh, x]
    id_copies = []
    for d in range(NX):
        dest = over_h * NX + (x + d) % NX
        id_copies.append(remote(own_ids, own_ids, si, NX + d, over_row, dest))
    for d in range(1, NX):
        id_copies.append(remote(own_ids, own_ids, si, d, row, rep_x(d)))
    for copy in id_copies:
        copy.start()
    a_copies = []
    for d in range(1, nq):
        copy = remote(rows_for(q_at(d)), cand.at[q], sa, d, row_q(d), rep)
        copy.start()
        a_copies.append(copy)
    own_copy = pltpu.make_async_copy(rows_for(q), cand.at[q], local_sem.at[2])
    own_copy.start()
    for d in close:
        r, p = z_dev(d)
        pl.semaphore_signal(
            far_sem, inc=1, device_id={"row": r, "rep": p}, device_id_type=MESH
        )
    own_copy.wait()
    for copy in id_copies + a_copies:
        copy.wait_recv()
    pending += id_copies + a_copies

    def wanted(h, t, k):
        first = ids[h, t].astype(F32)[k * share_rows : k * share_rows + 1]
        full = jnp.broadcast_to(first, ids.shape[2:])
        group = jnp.floor(full * (1.0 / nq))
        return group.astype(BF16), (full - group * nq).astype(BF16)

    here = pl.ds(x * per_x, per_x)

    def give(d):
        return remote(
            pick.at[(x + d) % NX], pieces.at[:, :, here], sx, d, row, rep_x(d)
        )

    def choose(i, carry):
        d = (i + 1) % NX
        t = (x + d) % NX
        for h in range(NH):
            for k in range(section_count):
                want = wanted(h, t, k)[1][None]
                chosen = cand[0]
                for s in range(1, nq):
                    chosen = jnp.where(want == jnp.asarray(s, BF16), cand[s], chosen)
                pick[t, h, k] = chosen

        @pl.when(i < NX - 1)
        def _():
            give(d).start()

        return carry

    lax.fori_loop(0, NX, choose, 0)
    x_copies = [give(d) for d in range(1, NX)]
    pieces[:, :, here] = pick[x]
    for copy in x_copies:
        copy.wait_recv()
    pending += x_copies

    near = [d for n in range(half, 0, -1) for d in (-n, n) if d < half]
    r_copies = []
    for i, d in enumerate(near):
        r, p = z_dev(d)
        copy = remote(pieces.at[:, :, r // nq], zcand.at[zl], sr, i, r, p)
        copy.start()
        r_copies.append(copy)
    zcand[zl] = pieces[:, :, zl]
    for copy in r_copies:
        copy.wait_recv()
    pending += r_copies
    for h in range(NH):
        for k in range(section_count):
            want = wanted(h, x, k)[0]
            chosen = zcand[0, h, k]
            for s in range(1, NZ):
                chosen = jnp.where(want == jnp.asarray(s, BF16), zcand[s, h, k], chosen)
            held[h, k] = chosen

    g_copies = []
    for i, d in enumerate(near):
        r, p = z_dev(d)
        copy = remote(held.at[p // NX], gathered.at[:, q, zl], sg, i, r, p)
        copy.start()
        g_copies.append(copy)
    gathered[:, q, zl] = held[zh]
    for copy in g_copies:
        copy.wait_recv()
    pending += g_copies

    def y_step(dy):
        return q_at((dy % NY) * NC)

    def y_send(origin, dy, slot, only=None):
        ref = gathered.at[:, y_step(origin)]
        if only is not None:
            ref = gathered.at[only, y_step(origin)]
        copy = remote(ref, ref, sy, slot, zl * nq + y_step(dy), rep)
        copy.start()
        pending.append(copy)
        return copy

    c_copies = []

    def hand_on(dy):
        ref = gathered.at[:, y_step(dy)]
        copy = remote(ref, ref, sc, dy % NY, row_q(1), rep)
        copy.start()
        c_copies.append(copy)

    up2 = y_send(0, 2, 0)
    down2 = y_send(0, -2, 1)
    up1 = y_send(0, 1, 2)
    down1 = y_send(0, -1, 3)
    hand_on(0)
    up2.wait_recv()
    up4 = y_send(-2, 2, 4, 0)
    up3 = y_send(-2, 1, 5)
    hand_on(-2)
    down2.wait_recv()
    down4 = y_send(2, -2, 6, 1)
    down3 = y_send(2, -1, 7)
    hand_on(2)
    up1.wait_recv()
    hand_on(-1)
    down1.wait_recv()
    hand_on(1)
    up3.wait_recv()
    hand_on(-3)
    down3.wait_recv()
    hand_on(3)
    up4.wait_recv()
    down4.wait_recv()
    hand_on(4)
    for copy in c_copies:
        copy.wait_recv()
    pending += c_copies

    tile_copy.wait()
    per_owner = block_count // (NH * NX)
    edge = agg.shape[-1]

    def product(b):
        left, right = [], []
        for k in range(section_count):
            for m in range(slot_count):
                live = m < count_ref[k, b]
                col = jnp.where(live, column_ref[m, k, b], block_count)
                left.append(tiles[k, b, m])
                right.append(gathered[k, col].reshape(edge, edge))
        return jnp.dot(
            jnp.concatenate(left, axis=1),
            jnp.concatenate(right, axis=0),
            preferred_element_type=F32,
        )

    def share(stage, d):
        return remote(
            agg.at[stage, d], xsum.at[stage, d], sp, stage * NX + d, row, rep_x(d)
        )

    def summed_over_x(stage, h):
        def target(i, carry):
            d = (i + 1) % NX
            first = (h * NX + (x + d) % NX) * per_owner

            def one(j, inner):
                value = product(first + j)
                own[j] = value
                agg[stage, d, j] = value.astype(ROW_SUM)
                return inner

            lax.fori_loop(0, per_owner, one, 0)

            @pl.when(i < NX - 1)
            def _():
                share(stage, d).start()

            return carry

        lax.fori_loop(0, NX, target, 0)
        for d in range(1, NX):
            share(stage, d).wait_recv()
            pending.append(share(stage, d))
        out = own[...]
        for d in range(1, NX):
            out = out + xsum[stage, d].astype(F32)
        return out

    zsend[...] = summed_over_x(0, 1 - zh).astype(HALF_SUM)
    pl.semaphore_wait(far_sem, len(close))
    partner = z_dev(NZ)
    h_copy = remote(zsend, zsum, sh, 0, partner[0], partner[1])
    h_copy.start()
    kept = summed_over_x(1, zh)
    h_copy.wait_recv()
    pending.append(h_copy)
    summed = kept + zsum[...].astype(F32)
    aggregate = summed.reshape(own_rows, edge).astype(BF16)

    weight_copy.wait()
    preact = jnp.dot(aggregate, weight_ref[...], preferred_element_type=F32)
    sigmoid = jax.nn.sigmoid(preact)
    act_ref[...] = (preact * sigmoid).astype(BF16)
    slope = sigmoid * (1.0 + preact * (1.0 - sigmoid))
    cot_copy.wait()
    pre_grad = (cot[...].astype(F32) * slope).astype(BF16)
    part = lax.dot_general(
        aggregate, pre_grad, (((0,), (0,)), ((), ())), preferred_element_type=F32
    )
    tall, wide = wsend.shape[1:]
    across = part.shape[1] // wide
    for t in range(nq):
        top, left = (t // across) * tall, (t % across) * wide
        wsend[t] = part[top : top + tall, left : left + wide].astype(GRAD_A)

    w_copies = []
    for d in range(1, nq):
        copy = remote(wsend.at[q_at(d)], wrecv.at[q], sw, d, row_q(d), rep)
        copy.start()
        w_copies.append(copy)
    wrecv[q] = wsend[q]
    for copy in w_copies:
        copy.wait_recv()
    pending += w_copies
    xgrad[x] = functools.reduce(
        lambda a, b: a + b, [wrecv[t].astype(F32) for t in range(nq)]
    ).astype(GRAD_B)
    v_copies = []
    for d in range(1, NX):
        copy = remote(xgrad.at[x], xgrad.at[x], sv, d, row, rep_x(d))
        copy.start()
        v_copies.append(copy)
    for copy in v_copies:
        copy.wait_recv()
    pending += v_copies
    zgrad[z] = functools.reduce(
        lambda a, b: a + b, [xgrad[t].astype(F32) for t in range(NX)]
    ).astype(GRAD_B)
    u_copies = []
    for d in range(1, NZ * NH):
        r, p = z_dev(d)
        copy = remote(zgrad.at[z], zgrad.at[z], su, d, r, p)
        copy.start()
        u_copies.append(copy)
    for copy in u_copies:
        copy.wait_recv()
    pending += u_copies
    wfull[q] = functools.reduce(
        lambda a, b: a + b, [zgrad[t].astype(F32) for t in range(NZ * NH)]
    ).astype(GRAD_B)
    o_copies = []
    for d in range(1, nq):
        copy = remote(wfull.at[q], wfull.at[q], so, d, row_q(d), rep)
        copy.start()
        o_copies.append(copy)
    for copy in o_copies:
        copy.wait_recv()
    pending += o_copies
    for t in range(nq):
        top, left = (t // across) * tall, (t % across) * wide
        grad_ref[top : top + tall, left : left + wide] = wfull[t].astype(F32)

    for copy in pending:
        copy.wait_send()


def body(features, weight, section_source, tile_columns, tile_counts, tile_values, cotangent):
    rows, width = features.shape
    sections, blocks, slots, edge, _ = tile_values.shape
    hidden = weight.shape[1]
    nq = NY * NC
    piece = edge // NZ
    own_rows = rows // (NH * NX)
    per_owner = blocks // (NH * NX)
    per_x = NZ // NX
    tall = width * (hidden // edge) // nq
    dma = pltpu.SemaphoreType.DMA
    counts = [nq, 2 * NX, NX, NZ, NZ, NY, NY, NH * NX, 1, nq, NX, NZ * NH, nq]
    smem = pl.BlockSpec(memory_space=pltpu.SMEM)
    vmem = pl.BlockSpec(memory_space=pltpu.VMEM)
    hbm = pl.BlockSpec(memory_space=pltpu.HBM)
    return pl.pallas_call(
        kernel,
        out_shape=(
            jax.ShapeDtypeStruct((own_rows, hidden), BF16),
            jax.ShapeDtypeStruct((width, hidden), F32),
        ),
        in_specs=[smem, smem, smem, hbm, hbm, hbm, hbm],
        out_specs=(vmem, vmem),
        scratch_shapes=[
            pltpu.VMEM(tile_values.shape, BF16),
            pltpu.VMEM((own_rows, hidden), BF16),
            pltpu.VMEM(weight.shape, BF16),
            pltpu.VMEM((NH, NX, piece, width), BF16),
            pltpu.VMEM((nq, per_x, piece, width), BF16),
            pltpu.VMEM((NX, NH, sections, per_x, piece, width), BF16),
            pltpu.VMEM((NH, sections, NZ, piece, width), BF16),
            pltpu.VMEM((NZ, NH, sections, piece, width), BF16),
            pltpu.VMEM((NH, sections, piece, width), BF16),
            pltpu.VMEM((sections, blocks + 1, NZ, piece, width), BF16),
            pltpu.VMEM((NH, NX, per_owner, edge, width), ROW_SUM),
            pltpu.VMEM((NH, NX, per_owner, edge, width), ROW_SUM),
            pltpu.VMEM((per_owner, edge, width), F32),
            pltpu.VMEM((per_owner, edge, width), HALF_SUM),
            pltpu.VMEM((per_owner, edge, width), HALF_SUM),
            pltpu.VMEM((nq, tall, edge), GRAD_A),
            pltpu.VMEM((nq, tall, edge), GRAD_A),
            pltpu.VMEM((NX, tall, edge), GRAD_B),
            pltpu.VMEM((NZ * NH, tall, edge), GRAD_B),
            pltpu.VMEM((nq, tall, edge), GRAD_B),
            dma((4,)),
            pltpu.SemaphoreType.REGULAR,
        ]
        + [dma((n,)) for n in counts for _ in range(2)],
        compiler_params=pltpu.CompilerParams(
            collective_id=0, has_side_effects=True, vmem_limit_bytes=62 * 1024 * 1024
        ),
        cost_estimate=pl.CostEstimate(
            flops=2 * sections * blocks * slots * edge * edge * width,
            bytes_accessed=tile_values.size * 2,
            transcendentals=own_rows * hidden,
        ),
    )(
        section_source,
        tile_columns.transpose(2, 0, 1),
        tile_counts,
        weight,
        features.reshape(rows // piece, piece, width),
        tile_values,
        cotangent,
    )


def solution(mesh):
    in_specs = (
        P("row", None),
        P(),
        P("rep"),
        P("rep", "row", None),
        P("rep", "row"),
        P("rep", "row", None, None, None),
        P("row", None),
    )
    out_specs = (P(("row", "rep"), None), P())
    return jax.shard_map(body, mesh=mesh, in_specs=in_specs, out_specs=out_specs, check_vma=False)
```

```python
import functools

import jax
import jax.numpy as jnp
from jax import lax
from jax.experimental import pallas as pl
from jax.experimental.pallas import tpu as pltpu
from jax.sharding import PartitionSpec as P

MESH = pl.DeviceIdType.MESH
BF16, F32 = jnp.bfloat16, jnp.float32

NZ, NY, NC, NH, NX = 8, 8, 2, 2, 4
ROW_SUM = BF16
HALF_SUM = BF16
GRAD_A = BF16
GRAD_B = F32


def remote(src, dst, sems, slot, row, rep):
    send, recv = sems
    return pltpu.make_async_remote_copy(
        src_ref=src,
        dst_ref=dst,
        send_sem=send.at[slot],
        recv_sem=recv.at[slot],
        device_id={"row": row, "rep": rep},
        device_id_type=MESH,
    )


def kernel(
    source_ref,
    column_ref,
    count_ref,
    weight_hbm,
    features_ref,
    tiles_ref,
    cotangent_ref,
    act_ref,
    grad_ref,
    tiles,
    cot,
    weight_ref,
    ids,
    cand,
    pick,
    pieces,
    zcand,
    held,
    gathered,
    agg,
    xsum,
    own,
    zsum,
    zsend,
    wsend,
    wrecv,
    xgrad,
    zgrad,
    wfull,
    local_sem,
    far_sem,
    *sems,
):
    nq = NY * NC
    section_count, block_count, slot_count = tiles.shape[:3]
    sa, si, sx, sr, sg, sy, sc, sp, sh, sw, sv, su, so = [
        (sems[2 * i], sems[2 * i + 1]) for i in range(13)
    ]
    row, rep = lax.axis_index("row"), lax.axis_index("rep")
    zl, q = row // nq, row % nq
    y, c = q // NC, q % NC
    zh, x = rep // NX, rep % NX
    z = zh * NZ + zl

    def q_at(d):
        dy, dc = d // NC, d % NC
        return ((y + dy) % NY) * NC + (c + dc) % NC

    q_far = sorted(range(1, nq), key=lambda d: -min(d // NC, NY - d // NC))
    z_far = sorted(range(1, NZ * NH), key=lambda d: -min(d, NZ * NH - d))

    def row_q(d):
        return zl * nq + q_at(d)

    def rep_x(d):
        return zh * NX + (x + d) % NX

    def z_pos(d):
        return (z + d + NZ * NH) % (NZ * NH)

    def z_dev(d):
        zz = z_pos(d)
        return (zz % NZ) * nq + q, (zz // NZ) * NX + x

    barrier = pltpu.get_barrier_semaphore()
    peers = [(row_q(d), rep) for d in q_far]
    peers += [(row, rep_x(d)) for d in range(1, NX)]
    half = NZ // 2
    close = [d for n in range(half, 0, -1) for d in (-n, n)]
    peers += [z_dev(d) for d in close]
    over = (zl // half) * NZ - half
    over_row, over_rep = z_dev(over)
    over_h = over_rep // NX
    peers += [(over_row, over_h * NX + (x + d) % NX) for d in range(1, NX)]
    for r, p in reversed(peers):
        pl.semaphore_signal(
            barrier, inc=1, device_id={"row": r, "rep": p}, device_id_type=MESH
        )

    tile_copy = pltpu.make_async_copy(tiles_ref, tiles, local_sem.at[0])
    tile_copy.start()
    own_rows = cot.shape[0]
    cot_copy = pltpu.make_async_copy(
        cotangent_ref.at[pl.ds(pl.multiple_of(rep * own_rows, own_rows), own_rows)],
        cot,
        local_sem.at[1],
    )
    cot_copy.start()
    weight_copy = pltpu.make_async_copy(weight_hbm, weight_ref, local_sem.at[3])
    weight_copy.start()

    piece = ids.shape[2]
    share_rows = piece // section_count
    which = lax.broadcasted_iota(jnp.int32, ids.shape[2:], 0) // share_rows
    mixed = jnp.zeros(ids.shape[2:], jnp.int32)
    for k in range(section_count):
        mixed = jnp.where(which == k, source_ref[k], mixed)
    ids[zh, x] = mixed.astype(F32).astype(BF16)
    gathered[:, block_count] = jnp.zeros(
        (section_count,) + gathered.shape[2:], BF16
    )

    pl.semaphore_wait(barrier, len(peers))

    pending = []

    per_x = NZ // NX

    def rows_for(dq):
        return features_ref.at[pl.ds(dq * NZ + x * per_x, per_x)]

    own_ids = ids.at[zh, x]
    id_copies = []
    for d in range(NX):
        dest = over_h * NX + (x + d) % NX
        id_copies.append(remote(own_ids, own_ids, si, NX + d, over_row, dest))
    for d in range(1, NX):
        id_copies.append(remote(own_ids, own_ids, si, d, row, rep_x(d)))
    for copy in id_copies:
        copy.start()
    a_copies = []
    for d in q_far:
        copy = remote(rows_for(q_at(d)), cand.at[q], sa, d, row_q(d), rep)
        copy.start()
        a_copies.append(copy)
    own_copy = pltpu.make_async_copy(rows_for(q), cand.at[q], local_sem.at[2])
    own_copy.start()
    for d in close:
        r, p = z_dev(d)
        pl.semaphore_signal(
            far_sem, inc=1, device_id={"row": r, "rep": p}, device_id_type=MESH
        )
    own_copy.wait()
    for copy in id_copies + a_copies:
        copy.wait_recv()
    pending += id_copies + a_copies

    def wanted(h, t, k):
        first = ids[h, t].astype(F32)[k * share_rows : k * share_rows + 1]
        full = jnp.broadcast_to(first, ids.shape[2:])
        group = jnp.floor(full * (1.0 / nq))
        return group.astype(BF16), (full - group * nq).astype(BF16)

    here = pl.ds(x * per_x, per_x)

    def give(d):
        return remote(
            pick.at[(x + d) % NX], pieces.at[:, :, here], sx, d, row, rep_x(d)
        )

    def choose(i, carry):
        d = (i + 1) % NX
        t = (x + d) % NX
        for h in range(NH):
            for k in range(section_count):
                want = wanted(h, t, k)[1][None]
                chosen = cand[0]
                for s in range(1, nq):
                    chosen = jnp.where(want == jnp.asarray(s, BF16), cand[s], chosen)
                pick[t, h, k] = chosen

        @pl.when(i < NX - 1)
        def _():
            give(d).start()

        return carry

    lax.fori_loop(0, NX, choose, 0)
    x_copies = [give(d) for d in range(1, NX)]
    pieces[:, :, here] = pick[x]
    for copy in x_copies:
        copy.wait_recv()
    pending += x_copies

    near = [d for n in range(half, 0, -1) for d in (-n, n) if d < half]
    r_copies = []
    for i, d in enumerate(near):
        r, p = z_dev(d)
        copy = remote(pieces.at[:, :, r // nq], zcand.at[zl], sr, i, r, p)
        copy.start()
        r_copies.append(copy)
    zcand[zl] = pieces[:, :, zl]
    for copy in r_copies:
        copy.wait_recv()
    pending += r_copies
    for h in range(NH):
        for k in range(section_count):
            want = wanted(h, x, k)[0]
            chosen = zcand[0, h, k]
            for s in range(1, NZ):
                chosen = jnp.where(want == jnp.asarray(s, BF16), zcand[s, h, k], chosen)
            held[h, k] = chosen

    g_copies = []
    for i, d in enumerate(near):
        r, p = z_dev(d)
        copy = remote(held.at[p // NX], gathered.at[:, q, zl], sg, i, r, p)
        copy.start()
        g_copies.append(copy)
    gathered[:, q, zl] = held[zh]
    for copy in g_copies:
        copy.wait_recv()
    pending += g_copies

    def y_step(dy):
        return q_at((dy % NY) * NC)

    def y_send(origin, dy, slot, only=None):
        ref = gathered.at[:, y_step(origin)]
        if only is not None:
            ref = gathered.at[only, y_step(origin)]
        copy = remote(ref, ref, sy, slot, zl * nq + y_step(dy), rep)
        copy.start()
        pending.append(copy)
        return copy

    c_copies = []

    def hand_on(dy):
        ref = gathered.at[:, y_step(dy)]
        copy = remote(ref, ref, sc, dy % NY, row_q(1), rep)
        copy.start()
        c_copies.append(copy)

    up2 = y_send(0, 2, 0)
    down2 = y_send(0, -2, 1)
    up1 = y_send(0, 1, 2)
    down1 = y_send(0, -1, 3)
    hand_on(0)
    up2.wait_recv()
    up4 = y_send(-2, 2, 4, 0)
    up3 = y_send(-2, 1, 5)
    hand_on(-2)
    down2.wait_recv()
    down4 = y_send(2, -2, 6, 1)
    down3 = y_send(2, -1, 7)
    hand_on(2)
    up1.wait_recv()
    hand_on(-1)
    down1.wait_recv()
    hand_on(1)
    up3.wait_recv()
    hand_on(-3)
    down3.wait_recv()
    hand_on(3)
    up4.wait_recv()
    down4.wait_recv()
    hand_on(4)
    for copy in c_copies:
        copy.wait_recv()
    pending += c_copies

    tile_copy.wait()
    per_owner = block_count // (NH * NX)
    edge = agg.shape[-1]

    def product(b):
        left, right = [], []
        for k in range(section_count):
            for m in range(slot_count):
                live = m < count_ref[k, b]
                col = jnp.where(live, column_ref[m, k, b], block_count)
                left.append(tiles[k, b, m])
                right.append(gathered[k, col].reshape(edge, edge))
        return jnp.dot(
            jnp.concatenate(left, axis=1),
            jnp.concatenate(right, axis=0),
            preferred_element_type=F32,
        )

    def share(stage, d):
        return remote(
            agg.at[stage, d], xsum.at[stage, d], sp, stage * NX + d, row, rep_x(d)
        )

    def summed_over_x(stage, h):
        def target(i, carry):
            d = (i + 1) % NX
            first = (h * NX + (x + d) % NX) * per_owner

            def one(j, inner):
                value = product(first + j)
                own[j] = value
                agg[stage, d, j] = value.astype(ROW_SUM)
                return inner

            lax.fori_loop(0, per_owner, one, 0)

            @pl.when(i < NX - 1)
            def _():
                share(stage, d).start()

            return carry

        lax.fori_loop(0, NX, target, 0)
        for d in range(1, NX):
            share(stage, d).wait_recv()
            pending.append(share(stage, d))
        out = own[...]
        for d in range(1, NX):
            out = out + xsum[stage, d].astype(F32)
        return out

    zsend[...] = summed_over_x(0, 1 - zh).astype(HALF_SUM)
    pl.semaphore_wait(far_sem, len(close))
    partner = z_dev(NZ)
    h_copy = remote(zsend, zsum, sh, 0, partner[0], partner[1])
    h_copy.start()
    kept = summed_over_x(1, zh)
    h_copy.wait_recv()
    pending.append(h_copy)
    summed = kept + zsum[...].astype(F32)
    aggregate = summed.reshape(own_rows, edge).astype(BF16)

    weight_copy.wait()
    preact = jnp.dot(aggregate, weight_ref[...], preferred_element_type=F32)
    sigmoid = jax.nn.sigmoid(preact)
    act_ref[...] = (preact * sigmoid).astype(BF16)
    slope = sigmoid * (1.0 + preact * (1.0 - sigmoid))
    cot_copy.wait()
    pre_grad = (cot[...].astype(F32) * slope).astype(BF16)
    part = lax.dot_general(
        aggregate, pre_grad, (((0,), (0,)), ((), ())), preferred_element_type=F32
    )
    tall, wide = wsend.shape[1:]
    across = part.shape[1] // wide
    for t in range(nq):
        top, left = (t // across) * tall, (t % across) * wide
        wsend[t] = part[top : top + tall, left : left + wide].astype(GRAD_A)

    w_copies = []
    for d in q_far:
        copy = remote(wsend.at[q_at(d)], wrecv.at[q], sw, d, row_q(d), rep)
        copy.start()
        w_copies.append(copy)
    wrecv[q] = wsend[q]
    for copy in w_copies:
        copy.wait_recv()
    pending += w_copies
    xgrad[x] = functools.reduce(
        lambda a, b: a + b, [wrecv[t].astype(F32) for t in range(nq)]
    ).astype(GRAD_B)
    v_copies = []
    for d in range(1, NX):
        copy = remote(xgrad.at[x], xgrad.at[x], sv, d, row, rep_x(d))
        copy.start()
        v_copies.append(copy)
    for copy in v_copies:
        copy.wait_recv()
    pending += v_copies
    zgrad[z] = functools.reduce(
        lambda a, b: a + b, [xgrad[t].astype(F32) for t in range(NX)]
    ).astype(GRAD_B)
    u_copies = []
    for d in z_far:
        r, p = z_dev(d)
        copy = remote(zgrad.at[z], zgrad.at[z], su, d, r, p)
        copy.start()
        u_copies.append(copy)
    for copy in u_copies:
        copy.wait_recv()
    pending += u_copies
    wfull[q] = functools.reduce(
        lambda a, b: a + b, [zgrad[t].astype(F32) for t in range(NZ * NH)]
    ).astype(GRAD_B)
    o_copies = []
    for d in q_far:
        copy = remote(wfull.at[q], wfull.at[q], so, d, row_q(d), rep)
        copy.start()
        o_copies.append(copy)
    for copy in o_copies:
        copy.wait_recv()
    pending += o_copies
    for t in range(nq):
        top, left = (t // across) * tall, (t % across) * wide
        grad_ref[top : top + tall, left : left + wide] = wfull[t].astype(F32)

    for copy in pending:
        copy.wait_send()


def body(features, weight, section_source, tile_columns, tile_counts, tile_values, cotangent):
    rows, width = features.shape
    sections, blocks, slots, edge, _ = tile_values.shape
    hidden = weight.shape[1]
    nq = NY * NC
    piece = edge // NZ
    own_rows = rows // (NH * NX)
    per_owner = blocks // (NH * NX)
    per_x = NZ // NX
    tall = width * (hidden // edge) // nq
    dma = pltpu.SemaphoreType.DMA
    counts = [nq, 2 * NX, NX, NZ, NZ, NY, NY, NH * NX, 1, nq, NX, NZ * NH, nq]
    smem = pl.BlockSpec(memory_space=pltpu.SMEM)
    vmem = pl.BlockSpec(memory_space=pltpu.VMEM)
    hbm = pl.BlockSpec(memory_space=pltpu.HBM)
    return pl.pallas_call(
        kernel,
        out_shape=(
            pltpu.VMEM((own_rows, hidden), BF16),
            pltpu.VMEM((width, hidden), F32),
        ),
        in_specs=[smem, smem, smem, hbm, hbm, hbm, hbm],
        out_specs=(vmem, vmem),
        scratch_shapes=[
            pltpu.VMEM(tile_values.shape, BF16),
            pltpu.VMEM((own_rows, hidden), BF16),
            pltpu.VMEM(weight.shape, BF16),
            pltpu.VMEM((NH, NX, piece, width), BF16),
            pltpu.VMEM((nq, per_x, piece, width), BF16),
            pltpu.VMEM((NX, NH, sections, per_x, piece, width), BF16),
            pltpu.VMEM((NH, sections, NZ, piece, width), BF16),
            pltpu.VMEM((NZ, NH, sections, piece, width), BF16),
            pltpu.VMEM((NH, sections, piece, width), BF16),
            pltpu.VMEM((sections, blocks + 1, NZ, piece, width), BF16),
            pltpu.VMEM((NH, NX, per_owner, edge, width), ROW_SUM),
            pltpu.VMEM((NH, NX, per_owner, edge, width), ROW_SUM),
            pltpu.VMEM((per_owner, edge, width), F32),
            pltpu.VMEM((per_owner, edge, width), HALF_SUM),
            pltpu.VMEM((per_owner, edge, width), HALF_SUM),
            pltpu.VMEM((nq, tall, edge), GRAD_A),
            pltpu.VMEM((nq, tall, edge), GRAD_A),
            pltpu.VMEM((NX, tall, edge), GRAD_B),
            pltpu.VMEM((NZ * NH, tall, edge), GRAD_B),
            pltpu.VMEM((nq, tall, edge), GRAD_B),
            dma((4,)),
            pltpu.SemaphoreType.REGULAR,
        ]
        + [dma((n,)) for n in counts for _ in range(2)],
        compiler_params=pltpu.CompilerParams(
            collective_id=0, has_side_effects=True, vmem_limit_bytes=62 * 1024 * 1024
        ),
        cost_estimate=pl.CostEstimate(
            flops=2 * sections * blocks * slots * edge * edge * width,
            bytes_accessed=tile_values.size * 2,
            transcendentals=own_rows * hidden,
        ),
    )(
        section_source,
        tile_columns.transpose(2, 0, 1),
        tile_counts,
        weight,
        features.reshape(rows // piece, piece, width),
        tile_values,
        cotangent,
    )


def solution(mesh):
    in_specs = (
        P("row", None),
        P(),
        P("rep"),
        P("rep", "row", None),
        P("rep", "row"),
        P("rep", "row", None, None, None),
        P("row", None),
    )
    out_specs = (P(("row", "rep"), None), P())
    return jax.shard_map(body, mesh=mesh, in_specs=in_specs, out_specs=out_specs, check_vma=False)
```

```python
import functools

import jax
import jax.numpy as jnp
from jax import lax
from jax.experimental import pallas as pl
from jax.experimental.pallas import tpu as pltpu
from jax.sharding import PartitionSpec as P

MESH = pl.DeviceIdType.MESH
BF16, F32 = jnp.bfloat16, jnp.float32

NZ, NY, NC, NH, NX = 8, 8, 2, 2, 4
ROW_SUM = BF16
HALF_SUM = BF16
GRAD_A = BF16
GRAD_B = F32


def remote(src, dst, sems, slot, row, rep):
    send, recv = sems
    return pltpu.make_async_remote_copy(
        src_ref=src,
        dst_ref=dst,
        send_sem=send.at[slot],
        recv_sem=recv.at[slot],
        device_id={"row": row, "rep": rep},
        device_id_type=MESH,
    )


def kernel(
    source_ref,
    column_ref,
    count_ref,
    weight_hbm,
    features_ref,
    tiles_ref,
    cotangent_ref,
    act_ref,
    grad_ref,
    tiles,
    cot,
    weight_ref,
    ids,
    cand,
    pick,
    pieces,
    zcand,
    held,
    gathered,
    agg,
    xsum,
    own,
    zsum,
    zsend,
    wsend,
    wrecv,
    xgrad,
    zgrad,
    wfull,
    local_sem,
    far_sem,
    *sems,
):
    nq = NY * NC
    section_count, block_count, slot_count = tiles.shape[:3]
    sa, si, sx, sr, sg, sy, sc, sp, sh, sw, sv, su, so = [
        (sems[2 * i], sems[2 * i + 1]) for i in range(13)
    ]
    row, rep = lax.axis_index("row"), lax.axis_index("rep")
    zl, q = row // nq, row % nq
    y, c = q // NC, q % NC
    zh, x = rep // NX, rep % NX
    z = zh * NZ + zl

    def q_at(d):
        dy, dc = d // NC, d % NC
        return ((y + dy) % NY) * NC + (c + dc) % NC

    q_far = sorted(range(1, nq), key=lambda d: -min(d // NC, NY - d // NC))
    z_far = sorted(range(1, NZ * NH), key=lambda d: -min(d, NZ * NH - d))

    def row_q(d):
        return zl * nq + q_at(d)

    def rep_x(d):
        return zh * NX + (x + d) % NX

    def x_order(i):
        if NX != 4:
            return (i + 1) % NX
        late = i // 2
        return late * (3 - i) + (1 - late) * (i + 2)

    def z_pos(d):
        return (z + d + NZ * NH) % (NZ * NH)

    def z_dev(d):
        zz = z_pos(d)
        return (zz % NZ) * nq + q, (zz // NZ) * NX + x

    barrier = pltpu.get_barrier_semaphore()
    peers = [(row_q(d), rep) for d in q_far]
    peers += [(row, rep_x(d)) for d in range(1, NX)]
    half = NZ // 2
    close = [d for n in range(half, 0, -1) for d in (-n, n)]
    peers += [z_dev(d) for d in close]
    over = (zl // half) * NZ - half
    over_row, over_rep = z_dev(over)
    over_h = over_rep // NX
    peers += [(over_row, over_h * NX + (x + d) % NX) for d in range(1, NX)]
    for r, p in reversed(peers):
        pl.semaphore_signal(
            barrier, inc=1, device_id={"row": r, "rep": p}, device_id_type=MESH
        )

    tile_copy = pltpu.make_async_copy(tiles_ref, tiles, local_sem.at[0])
    tile_copy.start()
    own_rows = cot.shape[0]
    cot_copy = pltpu.make_async_copy(
        cotangent_ref.at[pl.ds(pl.multiple_of(rep * own_rows, own_rows), own_rows)],
        cot,
        local_sem.at[1],
    )
    cot_copy.start()
    weight_copy = pltpu.make_async_copy(weight_hbm, weight_ref, local_sem.at[3])
    weight_copy.start()

    piece = ids.shape[2]
    share_rows = piece // section_count
    which = lax.broadcasted_iota(jnp.int32, ids.shape[2:], 0) // share_rows
    mixed = jnp.zeros(ids.shape[2:], jnp.int32)
    for k in range(section_count):
        mixed = jnp.where(which == k, source_ref[k], mixed)
    ids[zh, x] = mixed.astype(F32).astype(BF16)
    gathered[:, block_count] = jnp.zeros(
        (section_count,) + gathered.shape[2:], BF16
    )

    pl.semaphore_wait(barrier, len(peers))

    pending = []

    per_x = NZ // NX

    def rows_for(dq):
        return features_ref.at[pl.ds(dq * NZ + x * per_x, per_x)]

    own_ids = ids.at[zh, x]
    id_copies = []
    for d in range(NX):
        dest = over_h * NX + (x + d) % NX
        id_copies.append(remote(own_ids, own_ids, si, NX + d, over_row, dest))
    for d in range(1, NX):
        id_copies.append(remote(own_ids, own_ids, si, d, row, rep_x(d)))
    for copy in id_copies:
        copy.start()
    a_copies = []
    for d in q_far:
        copy = remote(rows_for(q_at(d)), cand.at[q], sa, d, row_q(d), rep)
        copy.start()
        a_copies.append(copy)
    own_copy = pltpu.make_async_copy(rows_for(q), cand.at[q], local_sem.at[2])
    own_copy.start()
    for d in close:
        r, p = z_dev(d)
        pl.semaphore_signal(
            far_sem, inc=1, device_id={"row": r, "rep": p}, device_id_type=MESH
        )
    own_copy.wait()
    for copy in id_copies + a_copies:
        copy.wait_recv()
    pending += id_copies + a_copies

    def wanted(h, t, k):
        first = ids[h, t].astype(F32)[k * share_rows : k * share_rows + 1]
        full = jnp.broadcast_to(first, ids.shape[2:])
        group = jnp.floor(full * (1.0 / nq))
        return group.astype(BF16), (full - group * nq).astype(BF16)

    here = pl.ds(x * per_x, per_x)

    def give(d):
        return remote(
            pick.at[(x + d) % NX], pieces.at[:, :, here], sx, d, row, rep_x(d)
        )

    def choose(i, carry):
        d = x_order(i)
        t = (x + d) % NX
        for h in range(NH):
            for k in range(section_count):
                want = wanted(h, t, k)[1][None]
                chosen = cand[0]
                for s in range(1, nq):
                    chosen = jnp.where(want == jnp.asarray(s, BF16), cand[s], chosen)
                pick[t, h, k] = chosen

        @pl.when(i < NX - 1)
        def _():
            give(d).start()

        return carry

    lax.fori_loop(0, NX, choose, 0)
    x_copies = [give(d) for d in range(1, NX)]
    pieces[:, :, here] = pick[x]
    for copy in x_copies:
        copy.wait_recv()
    pending += x_copies

    near = [d for n in range(half, 0, -1) for d in (-n, n) if d < half]
    r_copies = []
    for i, d in enumerate(near):
        r, p = z_dev(d)
        copy = remote(pieces.at[:, :, r // nq], zcand.at[zl], sr, i, r, p)
        copy.start()
        r_copies.append(copy)
    zcand[zl] = pieces[:, :, zl]
    for copy in r_copies:
        copy.wait_recv()
    pending += r_copies
    for h in range(NH):
        for k in range(section_count):
            want = wanted(h, x, k)[0]
            chosen = zcand[0, h, k]
            for s in range(1, NZ):
                chosen = jnp.where(want == jnp.asarray(s, BF16), zcand[s, h, k], chosen)
            held[h, k] = chosen

    g_copies = []
    for i, d in enumerate(near):
        r, p = z_dev(d)
        copy = remote(held.at[p // NX], gathered.at[:, q, zl], sg, i, r, p)
        copy.start()
        g_copies.append(copy)
    gathered[:, q, zl] = held[zh]
    for copy in g_copies:
        copy.wait_recv()
    pending += g_copies

    def y_step(dy):
        return q_at((dy % NY) * NC)

    def y_send(origin, dy, slot, only=None):
        ref = gathered.at[:, y_step(origin)]
        if only is not None:
            ref = gathered.at[only, y_step(origin)]
        copy = remote(ref, ref, sy, slot, zl * nq + y_step(dy), rep)
        copy.start()
        pending.append(copy)
        return copy

    c_copies = []

    def hand_on(dy):
        ref = gathered.at[:, y_step(dy)]
        copy = remote(ref, ref, sc, dy % NY, row_q(1), rep)
        copy.start()
        c_copies.append(copy)

    up2 = y_send(0, 2, 0)
    down2 = y_send(0, -2, 1)
    up1 = y_send(0, 1, 2)
    down1 = y_send(0, -1, 3)
    hand_on(0)
    up2.wait_recv()
    up4 = y_send(-2, 2, 4, 0)
    up3 = y_send(-2, 1, 5)
    hand_on(-2)
    down2.wait_recv()
    down4 = y_send(2, -2, 6, 1)
    down3 = y_send(2, -1, 7)
    hand_on(2)
    up1.wait_recv()
    hand_on(-1)
    down1.wait_recv()
    hand_on(1)
    up3.wait_recv()
    hand_on(-3)
    down3.wait_recv()
    hand_on(3)
    up4.wait_recv()
    down4.wait_recv()
    hand_on(4)
    for copy in c_copies:
        copy.wait_recv()
    pending += c_copies

    tile_copy.wait()
    per_owner = block_count // (NH * NX)
    edge = agg.shape[-1]

    def product(b):
        left, right = [], []
        for k in range(section_count):
            for m in range(slot_count):
                live = m < count_ref[k, b]
                col = jnp.where(live, column_ref[m, k, b], block_count)
                left.append(tiles[k, b, m])
                right.append(gathered[k, col].reshape(edge, edge))
        return jnp.dot(
            jnp.concatenate(left, axis=1),
            jnp.concatenate(right, axis=0),
            preferred_element_type=F32,
        )

    def share(stage, d):
        return remote(
            agg.at[stage, d], xsum.at[stage, d], sp, stage * NX + d, row, rep_x(d)
        )

    def summed_over_x(stage, h):
        def target(i, carry):
            d = x_order(i)
            first = (h * NX + (x + d) % NX) * per_owner

            def one(j, inner):
                value = product(first + j)
                own[j] = value
                agg[stage, d, j] = value.astype(ROW_SUM)
                return inner

            lax.fori_loop(0, per_owner, one, 0)

            @pl.when(i < NX - 1)
            def _():
                share(stage, d).start()

            return carry

        lax.fori_loop(0, NX, target, 0)
        for d in range(1, NX):
            share(stage, d).wait_recv()
            pending.append(share(stage, d))

    def total(stage, j):
        out = own[j]
        for d in range(1, NX):
            out = out + xsum[stage, d, j].astype(F32)
        return out

    summed_over_x(0, 1 - zh)
    pl.semaphore_wait(far_sem, len(close))
    partner = z_dev(NZ)
    h_copies = []
    for j in range(per_owner):
        zsend[j] = total(0, j).astype(HALF_SUM)
        copy = remote(zsend.at[j], zsum.at[j], sh, j, partner[0], partner[1])
        copy.start()
        h_copies.append(copy)
    summed_over_x(1, zh)
    kept = [total(1, j) for j in range(per_owner)]
    for copy in h_copies:
        copy.wait_recv()
    pending += h_copies
    summed = jnp.stack([kept[j] + zsum[j].astype(F32) for j in range(per_owner)])
    aggregate = summed.reshape(own_rows, edge).astype(BF16)

    weight_copy.wait()
    preact = jnp.dot(aggregate, weight_ref[...], preferred_element_type=F32)
    sigmoid = jax.nn.sigmoid(preact)
    slope = sigmoid * (1.0 + preact * (1.0 - sigmoid))
    cot_copy.wait()
    pre_grad = (cot[...].astype(F32) * slope).astype(BF16)
    part = lax.dot_general(
        aggregate, pre_grad, (((0,), (0,)), ((), ())), preferred_element_type=F32
    )
    tall, wide = wsend.shape[1:]
    across = part.shape[1] // wide
    for t in range(nq):
        top, left = (t // across) * tall, (t % across) * wide
        wsend[t] = part[top : top + tall, left : left + wide].astype(GRAD_A)

    w_copies = []
    for d in q_far:
        copy = remote(wsend.at[q_at(d)], wrecv.at[q], sw, d, row_q(d), rep)
        copy.start()
        w_copies.append(copy)
    act_ref[...] = (preact * sigmoid).astype(BF16)
    wrecv[q] = wsend[q]
    for copy in w_copies:
        copy.wait_recv()
    pending += w_copies
    xgrad[x] = functools.reduce(
        lambda a, b: a + b, [wrecv[t].astype(F32) for t in range(nq)]
    ).astype(GRAD_B)
    v_copies = []
    for d in range(1, NX):
        copy = remote(xgrad.at[x], xgrad.at[x], sv, d, row, rep_x(d))
        copy.start()
        v_copies.append(copy)
    for copy in v_copies:
        copy.wait_recv()
    pending += v_copies
    zgrad[z] = functools.reduce(
        lambda a, b: a + b, [xgrad[t].astype(F32) for t in range(NX)]
    ).astype(GRAD_B)
    u_copies = []
    for d in z_far:
        r, p = z_dev(d)
        copy = remote(zgrad.at[z], zgrad.at[z], su, d, r, p)
        copy.start()
        u_copies.append(copy)
    for copy in u_copies:
        copy.wait_recv()
    pending += u_copies
    wfull[q] = functools.reduce(
        lambda a, b: a + b, [zgrad[t].astype(F32) for t in range(NZ * NH)]
    ).astype(GRAD_B)
    o_copies = []
    for d in q_far:
        copy = remote(wfull.at[q], wfull.at[q], so, d, row_q(d), rep)
        copy.start()
        o_copies.append(copy)
    for copy in o_copies:
        copy.wait_recv()
    pending += o_copies
    for t in range(nq):
        top, left = (t // across) * tall, (t % across) * wide
        grad_ref[top : top + tall, left : left + wide] = wfull[t].astype(F32)

    for copy in pending:
        copy.wait_send()


def body(features, weight, section_source, tile_columns, tile_counts, tile_values, cotangent):
    rows, width = features.shape
    sections, blocks, slots, edge, _ = tile_values.shape
    hidden = weight.shape[1]
    nq = NY * NC
    piece = edge // NZ
    own_rows = rows // (NH * NX)
    per_owner = blocks // (NH * NX)
    per_x = NZ // NX
    tall = width * (hidden // edge) // nq
    dma = pltpu.SemaphoreType.DMA
    counts = [nq, 2 * NX, NX, NZ, NZ, NY, NY, NH * NX, per_owner, nq, NX, NZ * NH, nq]
    smem = pl.BlockSpec(memory_space=pltpu.SMEM)
    vmem = pl.BlockSpec(memory_space=pltpu.VMEM)
    hbm = pl.BlockSpec(memory_space=pltpu.HBM)
    return pl.pallas_call(
        kernel,
        out_shape=(
            pltpu.VMEM((own_rows, hidden), BF16),
            pltpu.VMEM((width, hidden), F32),
        ),
        in_specs=[smem, smem, smem, hbm, hbm, hbm, hbm],
        out_specs=(vmem, vmem),
        scratch_shapes=[
            pltpu.VMEM(tile_values.shape, BF16),
            pltpu.VMEM((own_rows, hidden), BF16),
            pltpu.VMEM(weight.shape, BF16),
            pltpu.VMEM((NH, NX, piece, width), BF16),
            pltpu.VMEM((nq, per_x, piece, width), BF16),
            pltpu.VMEM((NX, NH, sections, per_x, piece, width), BF16),
            pltpu.VMEM((NH, sections, NZ, piece, width), BF16),
            pltpu.VMEM((NZ, NH, sections, piece, width), BF16),
            pltpu.VMEM((NH, sections, piece, width), BF16),
            pltpu.VMEM((sections, blocks + 1, NZ, piece, width), BF16),
            pltpu.VMEM((NH, NX, per_owner, edge, width), ROW_SUM),
            pltpu.VMEM((NH, NX, per_owner, edge, width), ROW_SUM),
            pltpu.VMEM((per_owner, edge, width), F32),
            pltpu.VMEM((per_owner, edge, width), HALF_SUM),
            pltpu.VMEM((per_owner, edge, width), HALF_SUM),
            pltpu.VMEM((nq, tall, edge), GRAD_A),
            pltpu.VMEM((nq, tall, edge), GRAD_A),
            pltpu.VMEM((NX, tall, edge), GRAD_B),
            pltpu.VMEM((NZ * NH, tall, edge), GRAD_B),
            pltpu.VMEM((nq, tall, edge), GRAD_B),
            dma((4,)),
            pltpu.SemaphoreType.REGULAR,
        ]
        + [dma((n,)) for n in counts for _ in range(2)],
        compiler_params=pltpu.CompilerParams(
            collective_id=0, has_side_effects=True, vmem_limit_bytes=62 * 1024 * 1024
        ),
        cost_estimate=pl.CostEstimate(
            flops=2 * sections * blocks * slots * edge * edge * width,
            bytes_accessed=tile_values.size * 2,
            transcendentals=own_rows * hidden,
        ),
    )(
        section_source,
        tile_columns.transpose(2, 0, 1),
        tile_counts,
        weight,
        features.reshape(rows // piece, piece, width),
        tile_values,
        cotangent,
    )


def solution(mesh):
    in_specs = (
        P("row", None),
        P(),
        P("rep"),
        P("rep", "row", None),
        P("rep", "row"),
        P("rep", "row", None, None, None),
        P("row", None),
    )
    out_specs = (P(("row", "rep"), None), P())
    return jax.shard_map(body, mesh=mesh, in_specs=in_specs, out_specs=out_specs, check_vma=False)
```
